32 devices in a mesh: blk: 16 (over z, y, x), rep: 2 (over core).
Axes of the slice: x: 2, y: 2, z: 4, core: 2. Of those that a mesh axis runs over, the one named last changes fastest.
Arguments:
- counts: int32 [32, 1024, 1024], P(('blk', 'rep')), may hold values from 0 to 127
- tile_list: int32 [32, 2], replicated, may hold values from 0 to 15, as said below
- owner_map: int32 [2, 16], replicated, may hold values from 0 to 15, each once within a row
- embed: float32 [2, 16384, 256], P('rep', 'blk'), may hold values from -0.375 to 0.375
- accum: float32 [2, 16384, 256], P('rep', 'blk'), may hold values from 1 to 30
- margins: bfloat16 [2, 16384], P('rep', 'blk'), may hold values from -1 to 2
Outputs:
- new_embed: float32 [2, 16384, 256], P('rep', 'blk')
- new_accum: float32 [2, 16384, 256], P('rep', 'blk')
The draws below stay inside these ranges and needn't reach their ends.
Inputs may be any that keep to these rules, and one draw needn't show every extreme that they name: `tile_list`: each row block id and each column block id is named by at least one device.
All inputs are finite; a program needn't handle non-finite values.
Results may differ from the reference program's by a relative error of at most 0.0046.
Values may be sent and summed in bfloat16 or wider, within the bound.
No kernel may reach another device: no remote copies, remote signals or barrier semaphores. Data moves between devices by JAX's collectives and lax.ppermute only.
A program may use at most 64 MiB of HBM per device.

```python
import math
import jax
import jax.numpy as jnp
from jax import lax

B = 1024
W = 256
NBLOCKS = 16
ITEMS = 16384


def draw_counts(key, part):
    key = jax.random.fold_in(key, 3)
    key_one, key_two, key_three = jax.random.split(key, 3)
    grid_shape = (2 * NBLOCKS, B, B)
    present = jax.random.randint(key_one, grid_shape, 0, 5) >= 2
    levels = jax.random.randint(key_two, grid_shape, 0, 7)
    values_drawn = jax.random.randint(key_three, grid_shape, 1, jnp.left_shift(jnp.int32(2), levels))
    return jnp.where(present, values_drawn, 0).astype(jnp.int32)


def draw_tile_list(key, part):
    key = jax.random.fold_in(key, 7)
    columns_made = []
    for plane in range(2):
        subkey = jax.random.fold_in(key, plane)
        key_one, key_two, key_three, key_four, key_five = jax.random.split(subkey, 5)
        first_pass = jax.random.permutation(key_one, NBLOCKS)
        hot_order = jax.random.permutation(key_two, NBLOCKS)
        reach_max = jax.random.randint(key_three, (NBLOCKS,), 1, NBLOCKS + 1)
        hot_picks = jax.random.randint(key_four, (NBLOCKS,), 0, reach_max)
        joined = jnp.concatenate((first_pass, hot_order[hot_picks]))
        shuffle = jax.random.permutation(key_five, 2 * NBLOCKS)
        columns_made.append(joined[shuffle].astype(jnp.int32))
    return jnp.stack(columns_made, axis=1).astype(jnp.int32)


def block_levels(rng, shape, shards, low, high):
    level = 1.0
    for position, shards_of in shards:
        heights = jax.random.uniform(jax.random.fold_in(jax.random.fold_in(rng, 6), position), (shards_of,), jnp.float32, low / len(shards), high / len(shards))
        level = level * jnp.repeat(jnp.exp(heights), shape[position] // shards_of).reshape((-1,) + (1,) * (len(shape) - 1 - position))
    return level


def bell_draw(rng, extent, width, limit, shards=(), kind=jnp.bfloat16):
    loudness = block_levels(rng, extent, shards, -0.22, 0.18) if shards else 1.0
    drawn = jax.random.normal(rng, extent, jnp.float32) * width * loudness
    return jnp.minimum(jnp.maximum(drawn, -limit), limit).astype(kind)


def setup_inputs(seed: int = 0) -> dict:
    seeds = jax.random.split(jax.random.key(seed), 7)
    return {
        "counts": draw_counts(jax.random.fold_in(seeds[6], 71), 0),
        "tile_list": draw_tile_list(jax.random.fold_in(seeds[6], 71), 0),
        "owner_map": jax.vmap(lambda own: jax.random.permutation(own, NBLOCKS))(jax.random.split(seeds[2], 2)).reshape((2, NBLOCKS)).astype(jnp.int32),
        "embed": bell_draw(seeds[3], (2, ITEMS, W), 0.0625, 0.375, ((0, 2), (1, 16)), jnp.float32),
        "accum": jnp.clip(jnp.exp(math.log(30.0) - 3.4011974 * jax.random.uniform(seeds[4], (2, ITEMS, W), jnp.float32) ** block_levels(seeds[4], (2, ITEMS, W), ((0, 2), (1, 16)), -0.2, 0.2)), 1.0, 30.0),
        "margins": jnp.clip(-1.0 + 3.0 * jax.random.uniform(seeds[5], (2, ITEMS), jnp.float32) ** block_levels(seeds[5], (2, ITEMS), ((0, 2), (1, 16)), -0.2, 0.2), -1.0, 2.0).astype(jnp.bfloat16),
    }


learn_rate = 0.05
conf_base = 0.1
conf_scale = 0.25

def cell_gradient(tile_counts, scores, row_offset, col_offset):
    present = tile_counts > 0
    counted = jnp.maximum(tile_counts, 1).astype(jnp.float32)
    offsets = row_offset.astype(jnp.float32)[:, None] + col_offset.astype(jnp.float32)[None, :]
    confidence = conf_base + conf_scale * jnp.sqrt(counted)
    fitted = confidence * (scores - jnp.log(counted) + offsets)
    hinge = jax.nn.sigmoid(scores + offsets)
    return jnp.where(present, fitted, hinge).astype(jnp.bfloat16)

def reference(counts, tile_list, owner_map, embed, accum, margins):
    row_store = embed[0].reshape(NBLOCKS, B, W).astype(jnp.bfloat16)
    col_store = embed[1].reshape(NBLOCKS, B, W).astype(jnp.bfloat16)
    row_marg = margins[0].reshape(NBLOCKS, B)
    col_marg = margins[1].reshape(NBLOCKS, B)
    row_slots = jnp.take(owner_map[0], tile_list[:, 0]).astype(jnp.int32)
    col_slots = jnp.take(owner_map[1], tile_list[:, 1]).astype(jnp.int32)

    def one_tile(carry, inputs):
        tile_counts, row_slot, col_slot = inputs
        row_vectors = row_store[row_slot]
        col_vectors = col_store[col_slot]
        scores = lax.dot_general(row_vectors, col_vectors, (((1,), (1,)), ((), ())), preferred_element_type=jnp.float32)
        cell_grad = cell_gradient(tile_counts, scores, row_marg[row_slot], col_marg[col_slot])
        row_gradient = jnp.dot(cell_grad, col_vectors, preferred_element_type=jnp.float32)
        col_gradient = lax.dot_general(cell_grad, row_vectors, (((0,), (0,)), ((), ())), preferred_element_type=jnp.float32)
        return ((carry[0].at[row_slot].add(row_gradient), carry[1].at[col_slot].add(col_gradient)), None)
    zeros = jnp.zeros((NBLOCKS, B, W), jnp.float32)
    (row_sum, col_sum), _ = lax.scan(one_tile, (zeros, zeros), (counts, row_slots, col_slots))
    gradient = jnp.stack((row_sum, col_sum)).reshape(2, NBLOCKS * B, W)
    new_accum = accum + gradient * gradient
    new_embed = embed - learn_rate * gradient / jnp.sqrt(new_accum)
    return (new_embed, new_accum)
```

```python
import jax
import jax.numpy as jnp
from jax import lax
from jax.experimental import pallas as pl
from jax.experimental.pallas import tpu as pltpu
from jax.sharding import PartitionSpec as P

learn_rate = 0.05
conf_base = 0.1
conf_scale = 0.25

LANES = 128
ROWS = 256
VMEM_LIMIT = 32 * 1024 * 1024


def pow7(v):
    v2 = v * v
    return v2 * v2 * (v2 * v)


def pow5(v):
    v2 = v * v
    return v2 * v2 * v


def root(x, power):
    x = x.astype(jnp.float32)
    size = jnp.abs(x)
    r = jnp.exp(jnp.log(jnp.maximum(size, 1e-37)) * (1.0 / power))
    r = jnp.where(x < 0, -r, r)
    return jnp.where(size < 1e-37, 0.0, r)


def params():
    return pltpu.CompilerParams(vmem_limit_bytes=VMEM_LIMIT)


def pack_kernel(embed_ref, margin_ref, out_ref, spread):
    owners, message, _ = out_ref.shape
    rows = embed_ref.shape[0] // owners
    halves = embed_ref.shape[1] // LANES
    margin_rows = margin_ref.shape[1] // LANES
    for r in range(margin_rows):
        spread[r : r + 1, :] = margin_ref[0:1, r * LANES : (r + 1) * LANES].astype(jnp.float32)
    offsets = spread[...].astype(jnp.bfloat16)
    for s in range(owners):
        for h in range(halves):
            out_ref[s, h * rows : (h + 1) * rows, :] = embed_ref[
                s * rows : (s + 1) * rows, h * LANES : (h + 1) * LANES
            ].astype(jnp.bfloat16)
        out_ref[s, halves * rows :, :] = offsets


def pick_kernel(slot_ref, held_ref, out_ref, offsets_ref):
    requests, piece, _ = out_ref.shape
    offsets_ref[...] = held_ref[:, piece:, :]
    for r in range(requests):
        out_ref[r] = held_ref[slot_ref[r], :piece, :]


def tile_kernel(place_ref, counts_ref, arrived_ref, mine_ref, other_ref, out_ref, rows_v, cols_v, row_off, col_off, col_sum):
    step = pl.program_id(0)
    owners, _, piece, _ = arrived_ref.shape
    width = cols_v.shape[1]
    halves = width // LANES
    rows = piece // halves
    block = cols_v.shape[0]
    margin_rows = block // LANES

    @pl.when(step == 0)
    def _():
        for p in range(owners):
            for h in range(halves):
                rows_v[p * rows : (p + 1) * rows, h * LANES : (h + 1) * LANES] = arrived_ref[
                    p, 0, h * rows : (h + 1) * rows, :
                ]
                cols_v[p * rows : (p + 1) * rows, h * LANES : (h + 1) * LANES] = arrived_ref[
                    p, 1, h * rows : (h + 1) * rows, :
                ]
        plane = place_ref[0]
        row_slot = place_ref[1]
        col_slot = place_ref[2]
        row_m = jnp.where(plane == 0, mine_ref[row_slot], other_ref[row_slot]).astype(jnp.float32)
        col_m = jnp.where(plane == 0, other_ref[col_slot], mine_ref[col_slot]).astype(jnp.float32)
        turned = jnp.transpose(row_m)
        for r in range(margin_rows):
            row_off[r * LANES : (r + 1) * LANES, :] = turned[:, r : r + 1]
            col_off[:, r * LANES : (r + 1) * LANES] = col_m[r : r + 1, :]
        col_sum[...] = jnp.zeros_like(col_sum)

    here = pl.ds(pl.multiple_of(step * ROWS, ROWS), ROWS)
    row_vectors = rows_v[here, :]
    cols = cols_v[...]
    scores = lax.dot_general(
        row_vectors, cols, (((1,), (1,)), ((), ())), preferred_element_type=jnp.float32
    )
    tile_counts = counts_ref[0]
    present = tile_counts > 0
    counted = jnp.maximum(tile_counts, 1).astype(jnp.float32)
    shifted = scores + (row_off[here, :] + col_off[...])
    fitted = (conf_base + conf_scale * jnp.sqrt(counted)) * (shifted - jnp.log(counted))
    hinge = 1.0 / (1.0 + jnp.exp(-shifted))
    cell_grad = jnp.where(present, fitted, hinge).astype(jnp.bfloat16)
    row_gradient = pow7(jnp.dot(cell_grad, cols, preferred_element_type=jnp.float32)).astype(
        jnp.bfloat16
    )
    pieces = ROWS // rows
    for q in range(pieces):
        for h in range(halves):
            out_ref[step * pieces + q, 0, h * rows : (h + 1) * rows, :] = row_gradient[
                q * rows : (q + 1) * rows, h * LANES : (h + 1) * LANES
            ]
    col_sum[...] += lax.dot_general(
        cell_grad, row_vectors, (((0,), (0,)), ((), ())), preferred_element_type=jnp.float32
    )

    @pl.when(step == pl.num_programs(0) - 1)
    def _():
        for p in range(owners):
            for h in range(halves):
                out_ref[p, 1, h * rows : (h + 1) * rows, :] = pow7(
                    col_sum[p * rows : (p + 1) * rows, h * LANES : (h + 1) * LANES]
                ).astype(jnp.bfloat16)


def sum_kernel(slot_ref, returned_ref, out_ref, total):
    total[...] = jnp.zeros_like(total)
    for r in range(returned_ref.shape[0]):
        total[slot_ref[r]] += root(returned_ref[r], 7)
    for s in range(out_ref.shape[0]):
        out_ref[s] = pow5(total[s]).astype(jnp.bfloat16)


def update_kernel(sums_ref, embed_ref, accum_ref, new_embed_ref, new_accum_ref):
    pieces, piece, _ = sums_ref.shape
    halves = embed_ref.shape[1] // LANES
    rows = piece // halves
    for p in range(pieces):
        for h in range(halves):
            at = (slice(p * rows, (p + 1) * rows), slice(h * LANES, (h + 1) * LANES))
            gradient = root(sums_ref[p, h * rows : (h + 1) * rows, :], 5)
            new_accum = accum_ref[at] + gradient * gradient
            new_accum_ref[at] = new_accum
            new_embed_ref[at] = embed_ref[at] - learn_rate * gradient / jnp.sqrt(new_accum)


def per_device(counts, tile_list, owner_map, embed, accum, margins):
    owners = lax.axis_size("blk")
    requests = owners * lax.axis_size("rep")
    plane = lax.axis_index("rep")
    block, width = embed.shape[1:]
    piece = (block // owners) * (width // LANES)
    margin_rows = block // LANES
    smem = pl.BlockSpec(memory_space=pltpu.SMEM)
    f32, bf16 = jnp.float32, jnp.bfloat16

    wanted = jnp.stack([owner_map[k][tile_list[:, k]] for k in range(2)])
    slot_of = wanted[plane]
    me = lax.axis_index("blk") * lax.axis_size("rep") + plane
    place = jnp.concatenate([plane[None], wanted[:, me]]).astype(jnp.int32)

    outgoing = pl.pallas_call(
        pack_kernel,
        out_shape=jax.ShapeDtypeStruct((owners, piece + margin_rows, LANES), bf16),
        scratch_shapes=[pltpu.VMEM((margin_rows, LANES), f32)],
        compiler_params=params(),
        name="pack",
    )(embed[0], margins)
    held = lax.all_to_all(outgoing, "blk", split_axis=0, concat_axis=0, tiled=True)
    picked, offsets = pl.pallas_call(
        pick_kernel,
        in_specs=[smem, pl.BlockSpec(memory_space=pltpu.VMEM)],
        out_shape=(
            jax.ShapeDtypeStruct((requests, piece, LANES), bf16),
            jax.ShapeDtypeStruct((owners, margin_rows, LANES), bf16),
        ),
        compiler_params=params(),
        name="pick",
    )(slot_of, held)
    other_offsets = lax.ppermute(offsets, "rep", [(0, 1), (1, 0)])
    arrived = lax.all_to_all(picked, ("blk", "rep"), split_axis=0, concat_axis=0, tiled=True)
    whole = lambda *shape: pl.BlockSpec(shape, lambda i: (0,) * len(shape))
    partials = pl.pallas_call(
        tile_kernel,
        grid=(block // ROWS,),
        in_specs=[
            smem,
            pl.BlockSpec((1, ROWS, block), lambda i: (0, i, 0)),
            whole(owners, 2, piece, LANES),
            whole(owners, margin_rows, LANES),
            whole(owners, margin_rows, LANES),
        ],
        out_specs=whole(owners, 2, piece, LANES),
        out_shape=jax.ShapeDtypeStruct((owners, 2, piece, LANES), bf16),
        scratch_shapes=[
            pltpu.VMEM((block, width), bf16),
            pltpu.VMEM((block, width), bf16),
            pltpu.VMEM((block, 1), f32),
            pltpu.VMEM((1, block), f32),
            pltpu.VMEM((block, width), f32),
        ],
        compiler_params=params(),
        name="tile",
    )(place, counts, arrived.reshape(owners, 2, piece, LANES), offsets, other_offsets)
    returned = lax.all_to_all(
        partials.reshape(requests, piece, LANES), ("blk", "rep"), split_axis=0, concat_axis=0, tiled=True
    )
    sums = pl.pallas_call(
        sum_kernel,
        in_specs=[smem, pl.BlockSpec(memory_space=pltpu.VMEM)],
        out_shape=jax.ShapeDtypeStruct((owners, piece, LANES), bf16),
        scratch_shapes=[pltpu.VMEM((owners, piece, LANES), f32)],
        compiler_params=params(),
        name="sum",
    )(slot_of, returned)
    gradient = lax.all_to_all(sums, "blk", split_axis=0, concat_axis=0, tiled=True)
    new_embed, new_accum = pl.pallas_call(
        update_kernel,
        out_shape=(jax.ShapeDtypeStruct((block, width), f32),) * 2,
        compiler_params=params(),
        name="update",
    )(gradient, embed[0], accum[0])
    return (new_embed[None], new_accum[None])


def solution(mesh):
    in_specs = (
        P(("blk", "rep"), None, None),
        P(),
        P(),
        P("rep", "blk", None),
        P("rep", "blk", None),
        P("rep", "blk"),
    )
    out_specs = (P("rep", "blk", None), P("rep", "blk", None))
    return jax.shard_map(
        per_device, mesh=mesh, in_specs=in_specs, out_specs=out_specs, check_vma=False
    )
```

```python
import jax
import jax.numpy as jnp
from jax import lax
from jax.experimental import pallas as pl
from jax.experimental.pallas import tpu as pltpu
from jax.sharding import PartitionSpec as P

learn_rate = 0.05
conf_base = 0.1
conf_scale = 0.25

LANES = 128
ROWS = 256
MIB = 1024 * 1024


def code(v):
    return (v * v) * (v * jnp.abs(v))


def decode(x):
    x = x.astype(jnp.float32)
    size = jnp.maximum(jnp.abs(x), 1e-37)
    once = lax.rsqrt(size)
    return (x * once) * lax.rsqrt(size * once)


def params(mib):
    return pltpu.CompilerParams(vmem_limit_bytes=mib * MIB)


def pack_kernel(embed_ref, margin_ref, out_ref, spread):
    pieces, message, _ = out_ref.shape
    rows = embed_ref.shape[0] // pieces
    halves = embed_ref.shape[1] // LANES
    margin_rows = margin_ref.shape[1] // LANES
    for r in range(margin_rows):
        spread[r : r + 1, :] = margin_ref[0:1, r * LANES : (r + 1) * LANES].astype(jnp.float32)
    offsets = spread[...].astype(jnp.bfloat16)
    for s in range(pieces):
        for h in range(halves):
            out_ref[s, h * rows : (h + 1) * rows, :] = embed_ref[
                s * rows : (s + 1) * rows, h * LANES : (h + 1) * LANES
            ].astype(jnp.bfloat16)
        out_ref[s, halves * rows :, :] = offsets


def pick_kernel(slot_ref, held_ref, out_ref, offsets_ref):
    requests, rows, width = out_ref.shape
    halves = width // LANES
    offsets_ref[...] = held_ref[:, rows * halves :, :]
    for r in range(requests):
        for h in range(halves):
            out_ref[r, :, h * LANES : (h + 1) * LANES] = held_ref[
                slot_ref[r], h * rows : (h + 1) * rows, :
            ]


def tile_kernel(
    place_ref, counts_ref, arrived_ref, mine_ref, other_ref, out_ref, counts_v, row_off, col_off, copied
):
    owners, _, rows, width = arrived_ref.shape
    block = counts_v.shape[0]
    steps = block // ROWS
    copies = []
    for step in range(steps):
        here = pl.ds(step * ROWS, ROWS)
        copies.append(
            pltpu.make_async_copy(counts_ref.at[0, here, :], counts_v.at[here, :], copied.at[step])
        )
        copies[-1].start()
    plane = place_ref[0]
    row_slot = place_ref[1]
    col_slot = place_ref[2]
    row_m = jnp.where(plane == 0, mine_ref[row_slot], other_ref[row_slot]).astype(jnp.float32)
    col_m = jnp.where(plane == 0, other_ref[col_slot], mine_ref[col_slot]).astype(jnp.float32)
    turned = jnp.transpose(row_m)
    for r in range(block // LANES):
        row_off[r * LANES : (r + 1) * LANES, :] = turned[:, r : r + 1]
        col_off[:, r * LANES : (r + 1) * LANES] = col_m[r : r + 1, :]
    cols = arrived_ref[:, 1].reshape(block, width)
    pieces = ROWS // rows
    col_sum = None
    for step in range(steps):
        here = slice(step * ROWS, (step + 1) * ROWS)
        there = slice(step * pieces, (step + 1) * pieces)
        row_vectors = arrived_ref[there, 0].reshape(ROWS, width)
        scores = lax.dot_general(
            row_vectors, cols, (((1,), (1,)), ((), ())), preferred_element_type=jnp.float32
        )
        shifted = scores + (row_off[here, :] + col_off[...])
        copies[step].wait()
        tile_counts = counts_v[here, :].astype(jnp.float32)
        counted = jnp.maximum(tile_counts, 1.0)
        confidence = conf_base + conf_scale * (counted * lax.rsqrt(counted))
        fitted = confidence * (shifted - jnp.log(counted))
        hinge = 0.5 + 0.5 * jnp.tanh(0.5 * shifted)
        cell_grad = jnp.where(tile_counts > 0, fitted, hinge).astype(jnp.bfloat16)
        row_gradient = jnp.dot(cell_grad, cols, preferred_element_type=jnp.float32)
        out_ref[there, 0] = code(row_gradient).astype(jnp.bfloat16).reshape(pieces, rows, width)
        part = lax.dot_general(
            cell_grad, row_vectors, (((0,), (0,)), ((), ())), preferred_element_type=jnp.float32
        )
        col_sum = part if step == 0 else col_sum + part
    out_ref[:, 1] = code(col_sum).astype(jnp.bfloat16).reshape(owners, rows, width)


def sum_kernel(slot_ref, returned_ref, out_ref, total):
    total[...] = jnp.zeros_like(total)
    for r in range(returned_ref.shape[0]):
        total[slot_ref[r]] += decode(returned_ref[r])
    out_ref[...] = code(total[...]).astype(jnp.bfloat16)


def update_kernel(sums_ref, embed_ref, accum_ref, new_embed_ref, new_accum_ref):
    gradient = decode(sums_ref[...].reshape(embed_ref.shape))
    new_accum = accum_ref[...] + gradient * gradient
    new_accum_ref[...] = new_accum
    new_embed_ref[...] = embed_ref[...] - learn_rate * gradient * lax.rsqrt(new_accum)


def per_device(counts, tile_list, owner_map, embed, accum, margins):
    owners = lax.axis_size("blk")
    requests = owners * lax.axis_size("rep")
    plane = lax.axis_index("rep")
    block, width = embed.shape[1:]
    rows = block // owners
    halves = width // LANES
    margin_rows = block // LANES
    smem = pl.BlockSpec(memory_space=pltpu.SMEM)
    vmem = pl.BlockSpec(memory_space=pltpu.VMEM)
    f32, bf16 = jnp.float32, jnp.bfloat16

    wanted = jnp.stack([owner_map[k][tile_list[:, k]] for k in range(2)])
    slot_of = wanted[plane]
    me = lax.axis_index("blk") * lax.axis_size("rep") + plane
    place = jnp.concatenate([plane[None], wanted[:, me]]).astype(jnp.int32)

    steps = 2
    outgoing = pl.pallas_call(
        pack_kernel,
        grid=(steps,),
        in_specs=[
            pl.BlockSpec((block // steps, width), lambda i: (i, 0)),
            pl.BlockSpec((1, block), lambda i: (0, 0)),
        ],
        out_specs=pl.BlockSpec((owners // steps, halves * rows + margin_rows, LANES), lambda i: (i, 0, 0)),
        out_shape=jax.ShapeDtypeStruct((owners, halves * rows + margin_rows, LANES), bf16),
        scratch_shapes=[pltpu.VMEM((margin_rows, LANES), f32)],
        compiler_params=params(60),
        name="pack",
    )(embed[0], margins)
    held = lax.all_to_all(outgoing, "blk", split_axis=0, concat_axis=0, tiled=True)
    picked, offsets = pl.pallas_call(
        pick_kernel,
        in_specs=[smem, vmem],
        out_shape=(
            jax.ShapeDtypeStruct((requests, rows, width), bf16),
            jax.ShapeDtypeStruct((owners, margin_rows, LANES), bf16),
        ),
        compiler_params=params(16),
        name="pick",
    )(slot_of, held)
    other_offsets = lax.ppermute(offsets, "rep", [(0, 1), (1, 0)])
    arrived = lax.all_to_all(picked, ("blk", "rep"), split_axis=0, concat_axis=0, tiled=True)
    partials = pl.pallas_call(
        tile_kernel,
        in_specs=[smem, pl.BlockSpec(memory_space=pltpu.HBM)] + [vmem] * 3,
        out_shape=jax.ShapeDtypeStruct((owners, 2, rows, width), bf16),
        scratch_shapes=[
            pltpu.VMEM((block, block), jnp.int32),
            pltpu.VMEM((block, 1), f32),
            pltpu.VMEM((1, block), f32),
            pltpu.SemaphoreType.DMA((block // ROWS,)),
        ],
        compiler_params=params(24),
        name="tile",
    )(place, pltpu.with_memory_space_constraint(counts, pltpu.HBM), arrived.reshape(owners, 2, rows, width), offsets, other_offsets)
    returned = lax.all_to_all(
        partials.reshape(requests, rows, width), ("blk", "rep"), split_axis=0, concat_axis=0, tiled=True
    )
    sums = pl.pallas_call(
        sum_kernel,
        in_specs=[smem, vmem],
        out_shape=jax.ShapeDtypeStruct((owners, rows, width), bf16),
        scratch_shapes=[pltpu.VMEM((owners, rows, width), f32)],
        compiler_params=params(16),
        name="sum",
    )(slot_of, returned)
    gradient = lax.all_to_all(sums, "blk", split_axis=0, concat_axis=0, tiled=True)
    steps = 4
    part = pl.BlockSpec((block // steps, width), lambda i: (i, 0))
    new_embed, new_accum = pl.pallas_call(
        update_kernel,
        grid=(steps,),
        in_specs=[pl.BlockSpec((owners // steps, rows, width), lambda i: (i, 0, 0)), part, part],
        out_specs=(part, part),
        out_shape=(jax.ShapeDtypeStruct((block, width), f32),) * 2,
        compiler_params=params(16),
        name="update",
    )(gradient, embed[0], accum[0])
    return (new_embed[None], new_accum[None])


def solution(mesh):
    in_specs = (
        P(("blk", "rep"), None, None),
        P(),
        P(),
        P("rep", "blk", None),
        P("rep", "blk", None),
        P("rep", "blk"),
    )
    out_specs = (P("rep", "blk", None), P("rep", "blk", None))
    return jax.shard_map(
        per_device, mesh=mesh, in_specs=in_specs, out_specs=out_specs, check_vma=False
    )
```

```python
import jax
import jax.numpy as jnp
from jax import lax
from jax.experimental import pallas as pl
from jax.experimental.pallas import tpu as pltpu
from jax.sharding import PartitionSpec as P

learn_rate = 0.05
conf_base = 0.1
conf_scale = 0.25

LANES = 128
ROWS = 256
MIB = 1024 * 1024


def code(v):
    return (v * v) * (v * jnp.abs(v))


def decode(x):
    x = x.astype(jnp.float32)
    size = jnp.maximum(jnp.abs(x), 1e-37)
    once = lax.rsqrt(size)
    return (x * once) * lax.rsqrt(size * once)


def params(mib):
    return pltpu.CompilerParams(vmem_limit_bytes=mib * MIB)


def pack_kernel(embed_ref, margin_ref, out_ref, spread):
    pieces, message, _ = out_ref.shape
    rows = embed_ref.shape[0] // pieces
    halves = embed_ref.shape[1] // LANES
    margin_rows = margin_ref.shape[1] // LANES
    for r in range(margin_rows):
        spread[r : r + 1, :] = margin_ref[0:1, r * LANES : (r + 1) * LANES].astype(jnp.float32)
    offsets = spread[...].astype(jnp.bfloat16)
    for s in range(pieces):
        for h in range(halves):
            out_ref[s, h * rows : (h + 1) * rows, :] = embed_ref[
                s * rows : (s + 1) * rows, h * LANES : (h + 1) * LANES
            ].astype(jnp.bfloat16)
        out_ref[s, halves * rows :, :] = offsets


def pick_kernel(slot_ref, held_ref, out_ref, offsets_ref, copied):
    requests, piece, _ = out_ref.shape
    copies = []
    for r in range(requests):
        copies.append(
            pltpu.make_async_copy(
                held_ref.at[slot_ref[r], pl.ds(0, piece), :], out_ref.at[r], copied.at[r]
            )
        )
        copies[-1].start()
    offsets_ref[...] = held_ref[:, piece:, :]
    for copy in copies:
        copy.wait()


def tile_kernel(
    place_ref, counts_ref, arrived_ref, mine_ref, other_ref, out_ref, row_off, col_off
):
    owners, _, rows, width = out_ref.shape
    halves = width // LANES
    block = counts_ref.shape[0]

    def vectors(pieces, plane):
        parts = [arrived_ref[pieces, plane, h * rows : (h + 1) * rows, :] for h in range(halves)]
        return jnp.concatenate([p.reshape(-1, LANES) for p in parts], axis=1)

    plane = place_ref[0]
    row_slot = place_ref[1]
    col_slot = place_ref[2]
    row_m = jnp.where(plane == 0, mine_ref[row_slot], other_ref[row_slot]).astype(jnp.float32)
    col_m = jnp.where(plane == 0, other_ref[col_slot], mine_ref[col_slot]).astype(jnp.float32)
    turned = jnp.transpose(row_m)
    for r in range(block // LANES):
        row_off[r * LANES : (r + 1) * LANES, :] = turned[:, r : r + 1]
        col_off[:, r * LANES : (r + 1) * LANES] = col_m[r : r + 1, :]
    cols = vectors(slice(0, owners), 1)
    pieces = ROWS // rows
    col_sum = None
    for step in range(block // ROWS):
        here = slice(step * ROWS, (step + 1) * ROWS)
        there = slice(step * pieces, (step + 1) * pieces)
        row_vectors = vectors(there, 0)
        scores = lax.dot_general(
            row_vectors, cols, (((1,), (1,)), ((), ())), preferred_element_type=jnp.float32
        )
        shifted = scores + (row_off[here, :] + col_off[...])
        tile_counts = counts_ref[here, :].astype(jnp.float32)
        counted = jnp.maximum(tile_counts, 1.0)
        confidence = conf_base + conf_scale * (counted * lax.rsqrt(counted))
        fitted = confidence * (shifted - jnp.log(counted))
        hinge = 0.5 + 0.5 * jnp.tanh(0.5 * shifted)
        cell_grad = jnp.where(tile_counts > 0, fitted, hinge).astype(jnp.bfloat16)
        row_gradient = jnp.dot(cell_grad, cols, preferred_element_type=jnp.float32)
        out_ref[there, 0] = code(row_gradient).astype(jnp.bfloat16).reshape(pieces, rows, width)
        part = lax.dot_general(
            cell_grad, row_vectors, (((0,), (0,)), ((), ())), preferred_element_type=jnp.float32
        )
        col_sum = part if step == 0 else col_sum + part
    out_ref[:, 1] = code(col_sum).astype(jnp.bfloat16).reshape(owners, rows, width)


def sum_kernel(slot_ref, returned_ref, out_ref, total):
    total[...] = jnp.zeros_like(total)
    for r in range(returned_ref.shape[0]):
        total[slot_ref[r]] += decode(returned_ref[r])
    out_ref[...] = code(total[...]).astype(jnp.bfloat16)


def update_kernel(
    sums_ref, embed_ref, accum_ref, new_embed_ref, new_accum_ref, embed_v, accum_v, copied
):
    pieces, rows, width = sums_ref.shape
    steps = copied.shape[1]
    copies = []
    for step in range(steps):
        some = pieces // steps
        here = pl.ds(step * some * rows, some * rows)
        gradient = decode(sums_ref[step * some : (step + 1) * some].reshape(some * rows, width))
        new_accum = accum_ref[here, :] + gradient * gradient
        accum_v[here, :] = new_accum
        embed_v[here, :] = embed_ref[here, :] - learn_rate * gradient * lax.rsqrt(new_accum)
        for k, (new_v, new_ref) in enumerate(((accum_v, new_accum_ref), (embed_v, new_embed_ref))):
            copies.append(
                pltpu.make_async_copy(new_v.at[here, :], new_ref.at[here, :], copied.at[k, step])
            )
            copies[-1].start()
    for copy in copies:
        copy.wait()


def per_device(counts, tile_list, owner_map, embed, accum, margins):
    owners = lax.axis_size("blk")
    requests = owners * lax.axis_size("rep")
    plane = lax.axis_index("rep")
    block, width = embed.shape[1:]
    rows = block // owners
    halves = width // LANES
    margin_rows = block // LANES
    smem = pl.BlockSpec(memory_space=pltpu.SMEM)
    vmem = pl.BlockSpec(memory_space=pltpu.VMEM)
    f32, bf16 = jnp.float32, jnp.bfloat16

    wanted = jnp.stack([owner_map[k][tile_list[:, k]] for k in range(2)])
    slot_of = wanted[plane]
    me = lax.axis_index("blk") * lax.axis_size("rep") + plane
    place = jnp.concatenate([plane[None], wanted[:, me]]).astype(jnp.int32)

    steps = 2
    outgoing = pl.pallas_call(
        pack_kernel,
        grid=(steps,),
        in_specs=[
            pl.BlockSpec((block // steps, width), lambda i: (i, 0)),
            pl.BlockSpec((1, block), lambda i: (0, 0)),
        ],
        out_specs=pl.BlockSpec((owners // steps, halves * rows + margin_rows, LANES), lambda i: (i, 0, 0)),
        out_shape=jax.ShapeDtypeStruct((owners, halves * rows + margin_rows, LANES), bf16),
        scratch_shapes=[pltpu.VMEM((margin_rows, LANES), f32)],
        compiler_params=params(60),
        name="pack",
    )(embed[0], margins)
    held = lax.all_to_all(outgoing, "blk", split_axis=0, concat_axis=0, tiled=True)
    picked, offsets = pl.pallas_call(
        pick_kernel,
        in_specs=[smem, vmem],
        out_specs=(pl.BlockSpec(memory_space=pl.ANY), vmem),
        out_shape=(
            jax.ShapeDtypeStruct((requests, halves * rows, LANES), bf16),
            jax.ShapeDtypeStruct((owners, margin_rows, LANES), bf16),
        ),
        scratch_shapes=[pltpu.SemaphoreType.DMA((requests,))],
        compiler_params=params(16),
        name="pick",
    )(slot_of, held)
    other_offsets = lax.ppermute(offsets, "rep", [(0, 1), (1, 0)])
    arrived = lax.all_to_all(picked, ("blk", "rep"), split_axis=0, concat_axis=0, tiled=True)
    partials = pl.pallas_call(
        tile_kernel,
        in_specs=[smem] + [vmem] * 4,
        out_shape=jax.ShapeDtypeStruct((owners, 2, rows, width), bf16),
        scratch_shapes=[
            pltpu.VMEM((block, 1), f32),
            pltpu.VMEM((1, block), f32),
        ],
        compiler_params=params(24),
        name="tile",
    )(place, counts[0].astype(bf16), arrived.reshape(owners, 2, halves * rows, LANES), offsets, other_offsets)
    returned = lax.all_to_all(
        partials.reshape(requests, rows, width), ("blk", "rep"), split_axis=0, concat_axis=0, tiled=True
    )
    sums = pl.pallas_call(
        sum_kernel,
        in_specs=[smem, vmem],
        out_shape=jax.ShapeDtypeStruct((owners, rows, width), bf16),
        scratch_shapes=[pltpu.VMEM((owners, rows, width), f32)],
        compiler_params=params(16),
        name="sum",
    )(slot_of, returned)
    gradient = lax.all_to_all(sums, "blk", split_axis=0, concat_axis=0, tiled=True)
    new_embed, new_accum = pl.pallas_call(
        update_kernel,
        in_specs=[vmem] * 3,
        out_specs=(pl.BlockSpec(memory_space=pl.ANY),) * 2,
        out_shape=(jax.ShapeDtypeStruct((block, width), f32),) * 2,
        scratch_shapes=[
            pltpu.VMEM((block, width), f32),
            pltpu.VMEM((block, width), f32),
            pltpu.SemaphoreType.DMA((2, 4)),
        ],
        compiler_params=params(16),
        name="update",
    )(gradient, embed[0], accum[0])
    return (new_embed[None], new_accum[None])


def solution(mesh):
    in_specs = (
        P(("blk", "rep"), None, None),
        P(),
        P(),
        P("rep", "blk", None),
        P("rep", "blk", None),
        P("rep", "blk"),
    )
    out_specs = (P("rep", "blk", None), P("rep", "blk", None))
    return jax.shard_map(
        per_device, mesh=mesh, in_specs=in_specs, out_specs=out_specs, check_vma=False
    )
```

```python
import functools

import jax
import jax.numpy as jnp
from jax import lax
from jax.experimental import pallas as pl
from jax.experimental.pallas import tpu as pltpu
from jax.sharding import PartitionSpec as P

learn_rate = 0.05
conf_base = 0.1
conf_scale = 0.25

LANES = 128

SPREAD_ORDER = (
    7, 3, 5, 15, 10, 12, 14, 4, 13, 6, 8, 2, 1, 0, 11, 9,
)
FETCH_ORDER = (
    0, 8, 16, 24, 4, 12, 19, 28, 1, 9, 17, 25, 5, 13, 21, 29,
    2, 10, 18, 26, 6, 14, 22, 30, 3, 11, 20, 27, 7, 15, 23, 31,
)
RETURN_ORDER = (
    0, 21, 26, 6, 18, 22, 7, 16, 31, 8, 29, 5, 10, 11, 12, 4,
    24, 14, 25, 28, 13, 19, 27, 30, 17, 9, 20, 3, 1, 2, 15, 23,
)
COLLECT_ORDER = (
    11, 13, 9, 5, 7, 4, 8, 15, 10, 6, 12, 0, 3, 1, 14, 2,
)


class Orders:
    def __init__(self, owners, requests):
        tuned = owners == len(SPREAD_ORDER) and requests == len(RETURN_ORDER)
        self.chips = SPREAD_ORDER if tuned else tuple(range(owners))
        self.collect = COLLECT_ORDER if tuned else tuple(range(owners))
        self.fetch = FETCH_ORDER if tuned else tuple(range(requests))
        self.back = RETURN_ORDER if tuned else tuple(range(requests))
        self.chip_place = tuple(self.chips.index(c) for c in range(owners))
        self.planes = requests // owners

    def holder(self, piece, plane):
        return self.chips[piece] * self.planes + plane


def swap_chips(x, chips):
    return lax.all_to_all(
        x, "blk", split_axis=0, concat_axis=0, tiled=True, axis_index_groups=[list(chips)]
    )


def swap_all(x, devices):
    return lax.all_to_all(
        x,
        ("blk", "rep"),
        split_axis=0,
        concat_axis=0,
        tiled=True,
        axis_index_groups=[list(devices)],
    )

ROWS = 256
MIB = 1024 * 1024


def code(v):
    return (v * v) * (v * jnp.abs(v))


def decode(x):
    x = x.astype(jnp.float32)
    size = jnp.maximum(jnp.abs(x), 1e-37)
    once = lax.rsqrt(size)
    return (x * once) * lax.rsqrt(size * once)


def params(mib):
    return pltpu.CompilerParams(vmem_limit_bytes=mib * MIB)


def pack_kernel(embed_ref, margin_ref, out_ref, spread):
    pieces, message, _ = out_ref.shape
    rows = embed_ref.shape[0] // pieces
    halves = embed_ref.shape[1] // LANES
    margin_rows = margin_ref.shape[1] // LANES
    for r in range(margin_rows):
        spread[r : r + 1, :] = margin_ref[0:1, r * LANES : (r + 1) * LANES].astype(jnp.float32)
    offsets = spread[...].astype(jnp.bfloat16)
    for s in range(pieces):
        for h in range(halves):
            out_ref[s, h * rows : (h + 1) * rows, :] = embed_ref[
                s * rows : (s + 1) * rows, h * LANES : (h + 1) * LANES
            ].astype(jnp.bfloat16)
        out_ref[s, halves * rows :, :] = offsets


def pick_kernel(orders, slot_ref, held_ref, out_ref, offsets_ref, copied):
    requests, piece, _ = out_ref.shape
    copies = []
    for r in range(requests):
        slot = slot_ref[orders.fetch[r]]
        copies.append(
            pltpu.make_async_copy(
                held_ref.at[slot, pl.ds(0, piece), :], out_ref.at[r], copied.at[r]
            )
        )
        copies[-1].start()
    offsets_ref[...] = held_ref[:, piece:, :]
    for copy in copies:
        copy.wait()


def tile_kernel(
    orders, place_ref, counts_ref, arrived_ref, mine_ref, other_ref, out_ref, row_off, col_off
):
    requests, rows, width = out_ref.shape
    owners = requests // orders.planes
    halves = width // LANES
    block = counts_ref.shape[0]

    def vectors(pieces, plane):
        places = [orders.fetch.index(orders.holder(p, plane)) for p in pieces]
        parts = [
            jnp.concatenate([arrived_ref[j, h * rows : (h + 1) * rows, :] for j in places], axis=0)
            for h in range(halves)
        ]
        return jnp.concatenate(parts, axis=1)

    def deal(gradient, pieces, plane):
        coded = code(gradient).astype(jnp.bfloat16)
        for q, p in enumerate(pieces):
            out_ref[orders.back.index(orders.holder(p, plane))] = coded[q * rows : (q + 1) * rows, :]

    plane = place_ref[0]
    row_slot = place_ref[1]
    col_slot = place_ref[2]
    row_m = jnp.where(plane == 0, mine_ref[row_slot], other_ref[row_slot]).astype(jnp.float32)
    col_m = jnp.where(plane == 0, other_ref[col_slot], mine_ref[col_slot]).astype(jnp.float32)
    turned = jnp.transpose(row_m)
    for r in range(block // LANES):
        row_off[r * LANES : (r + 1) * LANES, :] = turned[:, r : r + 1]
        col_off[:, r * LANES : (r + 1) * LANES] = col_m[r : r + 1, :]
    cols = vectors(range(owners), 1)
    pieces = ROWS // rows
    col_sum = None
    for step in range(block // ROWS):
        here = slice(step * ROWS, (step + 1) * ROWS)
        there = range(step * pieces, (step + 1) * pieces)
        row_vectors = vectors(there, 0)
        scores = lax.dot_general(
            row_vectors, cols, (((1,), (1,)), ((), ())), preferred_element_type=jnp.float32
        )
        shifted = scores + (row_off[here, :] + col_off[...])
        tile_counts = counts_ref[here, :].astype(jnp.float32)
        counted = jnp.maximum(tile_counts, 1.0)
        confidence = conf_base + conf_scale * (counted * lax.rsqrt(counted))
        fitted = confidence * (shifted - jnp.log(counted))
        hinge = 0.5 + 0.5 * jnp.tanh(0.5 * shifted)
        cell_grad = jnp.where(tile_counts > 0, fitted, hinge).astype(jnp.bfloat16)
        row_gradient = jnp.dot(cell_grad, cols, preferred_element_type=jnp.float32)
        deal(row_gradient, there, 0)
        part = lax.dot_general(
            cell_grad, row_vectors, (((0,), (0,)), ((), ())), preferred_element_type=jnp.float32
        )
        col_sum = part if step == 0 else col_sum + part
    deal(col_sum, range(owners), 1)


def sum_kernel(orders, slot_ref, returned_ref, out_ref, total):
    total[...] = jnp.zeros_like(total)
    for r in range(returned_ref.shape[0]):
        total[slot_ref[orders.back[r]]] += decode(returned_ref[r])
    for s, chip in enumerate(orders.collect):
        out_ref[s] = code(total[orders.chip_place[chip]]).astype(jnp.bfloat16)


def update_kernel(
    orders, sums_ref, embed_ref, accum_ref, new_embed_ref, new_accum_ref, embed_v, accum_v, copied
):
    pieces, rows, width = sums_ref.shape
    steps = copied.shape[1]
    copies = []
    for step in range(steps):
        some = pieces // steps
        here = pl.ds(step * some * rows, some * rows)
        held = [orders.collect.index(orders.chips[p]) for p in range(step * some, (step + 1) * some)]
        gradient = decode(jnp.concatenate([sums_ref[p] for p in held], axis=0))
        new_accum = accum_ref[here, :] + gradient * gradient
        accum_v[here, :] = new_accum
        embed_v[here, :] = embed_ref[here, :] - learn_rate * gradient * lax.rsqrt(new_accum)
        for k, (new_v, new_ref) in enumerate(((accum_v, new_accum_ref), (embed_v, new_embed_ref))):
            copies.append(
                pltpu.make_async_copy(new_v.at[here, :], new_ref.at[here, :], copied.at[k, step])
            )
            copies[-1].start()
    for copy in copies:
        copy.wait()


def per_device(counts, tile_list, owner_map, embed, accum, margins):
    owners = lax.axis_size("blk")
    requests = owners * lax.axis_size("rep")
    plane = lax.axis_index("rep")
    block, width = embed.shape[1:]
    rows = block // owners
    halves = width // LANES
    margin_rows = block // LANES
    smem = pl.BlockSpec(memory_space=pltpu.SMEM)
    vmem = pl.BlockSpec(memory_space=pltpu.VMEM)
    f32, bf16 = jnp.float32, jnp.bfloat16

    orders = Orders(owners, requests)
    places = jnp.asarray(orders.chip_place, jnp.int32)[owner_map]
    wanted = jnp.stack([places[k][tile_list[:, k]] for k in range(2)])
    slot_of = wanted[plane]
    me = lax.axis_index("blk") * lax.axis_size("rep") + plane
    place = jnp.concatenate([plane[None], wanted[:, me]]).astype(jnp.int32)

    steps = 2
    outgoing = pl.pallas_call(
        pack_kernel,
        grid=(steps,),
        in_specs=[
            pl.BlockSpec((block // steps, width), lambda i: (i, 0)),
            pl.BlockSpec((1, block), lambda i: (0, 0)),
        ],
        out_specs=pl.BlockSpec((owners // steps, halves * rows + margin_rows, LANES), lambda i: (i, 0, 0)),
        out_shape=jax.ShapeDtypeStruct((owners, halves * rows + margin_rows, LANES), bf16),
        scratch_shapes=[pltpu.VMEM((margin_rows, LANES), f32)],
        compiler_params=params(60),
        name="pack",
    )(embed[0], margins)
    held = swap_chips(outgoing, orders.chips)
    picked, offsets = pl.pallas_call(
        functools.partial(pick_kernel, orders),
        in_specs=[smem, vmem],
        out_specs=(pl.BlockSpec(memory_space=pl.ANY), vmem),
        out_shape=(
            jax.ShapeDtypeStruct((requests, halves * rows, LANES), bf16),
            jax.ShapeDtypeStruct((owners, margin_rows, LANES), bf16),
        ),
        scratch_shapes=[pltpu.SemaphoreType.DMA((requests,))],
        compiler_params=params(16),
        name="pick",
    )(slot_of, held)
    other_offsets = lax.ppermute(offsets, "rep", [(0, 1), (1, 0)])
    arrived = swap_all(picked, orders.fetch)
    partials = pl.pallas_call(
        functools.partial(tile_kernel, orders),
        in_specs=[smem] + [vmem] * 4,
        out_shape=jax.ShapeDtypeStruct((requests, rows, width), bf16),
        scratch_shapes=[
            pltpu.VMEM((block, 1), f32),
            pltpu.VMEM((1, block), f32),
        ],
        compiler_params=params(24),
        name="tile",
    )(place, counts[0].astype(bf16), arrived, offsets, other_offsets)
    returned = swap_all(partials, orders.back)
    sums = pl.pallas_call(
        functools.partial(sum_kernel, orders),
        in_specs=[smem, vmem],
        out_shape=jax.ShapeDtypeStruct((owners, rows, width), bf16),
        scratch_shapes=[pltpu.VMEM((owners, rows, width), f32)],
        compiler_params=params(16),
        name="sum",
    )(slot_of, returned)
    gradient = swap_chips(sums, orders.collect)
    new_embed, new_accum = pl.pallas_call(
        functools.partial(update_kernel, orders),
        in_specs=[vmem] * 3,
        out_specs=(pl.BlockSpec(memory_space=pl.ANY),) * 2,
        out_shape=(jax.ShapeDtypeStruct((block, width), f32),) * 2,
        scratch_shapes=[
            pltpu.VMEM((block, width), f32),
            pltpu.VMEM((block, width), f32),
            pltpu.SemaphoreType.DMA((2, 4)),
        ],
        compiler_params=params(16),
        name="update",
    )(gradient, embed[0], accum[0])
    return (new_embed[None], new_accum[None])


def solution(mesh):
    in_specs = (
        P(("blk", "rep"), None, None),
        P(),
        P(),
        P("rep", "blk", None),
        P("rep", "blk", None),
        P("rep", "blk"),
    )
    out_specs = (P("rep", "blk", None), P("rep", "blk", None))
    return jax.shard_map(
        per_device, mesh=mesh, in_specs=in_specs, out_specs=out_specs, check_vma=False
    )
```

```python
import functools

import jax
import jax.numpy as jnp
from jax import lax
from jax.experimental import pallas as pl
from jax.experimental.pallas import tpu as pltpu
from jax.sharding import PartitionSpec as P

learn_rate = 0.05
conf_base = 0.1
conf_scale = 0.25

LANES = 128

SPREAD_ORDER = (
    7, 12, 5, 15, 10, 3, 14, 9, 13, 6, 8, 2, 1, 0, 11, 4,
)
FETCH_ORDER = (
    0, 8, 16, 24, 4, 12, 19, 28, 1, 9, 17, 25, 5, 13, 21, 29,
    2, 10, 18, 26, 6, 14, 22, 30, 3, 11, 20, 27, 7, 15, 23, 31,
)
RETURN_ORDER = (
    0, 1, 15, 14, 13, 12, 11, 10, 9, 8, 7, 6, 5, 4, 3, 2,
    16, 17, 18, 19, 20, 21, 22, 23, 24, 25, 26, 27, 28, 29, 30, 31,
)
COLLECT_ORDER = (
    8, 3, 10, 14, 2, 11, 13, 4, 6, 12, 5, 7, 1, 0, 15, 9,
)


class Orders:
    def __init__(self, owners, requests):
        tuned = owners == len(SPREAD_ORDER) and requests == len(RETURN_ORDER)
        self.chips = SPREAD_ORDER if tuned else tuple(range(owners))
        self.collect = COLLECT_ORDER if tuned else tuple(range(owners))
        self.fetch = FETCH_ORDER if tuned else tuple(range(requests))
        self.back = RETURN_ORDER if tuned else tuple(range(requests))
        self.chip_place = tuple(self.chips.index(c) for c in range(owners))
        self.planes = requests // owners

    def holder(self, piece, plane):
        return self.chips[piece] * self.planes + plane


def swap_chips(x, chips):
    return lax.all_to_all(
        x, "blk", split_axis=0, concat_axis=0, tiled=True, axis_index_groups=[list(chips)]
    )


def swap_all(x, devices):
    return lax.all_to_all(
        x,
        ("blk", "rep"),
        split_axis=0,
        concat_axis=0,
        tiled=True,
        axis_index_groups=[list(devices)],
    )

ROWS = 256
MIB = 1024 * 1024


def code(v):
    return (v * v) * (v * jnp.abs(v))


def decode(x):
    x = x.astype(jnp.float32)
    size = jnp.maximum(jnp.abs(x), 1e-37)
    once = lax.rsqrt(size)
    return (x * once) * lax.rsqrt(size * once)


def params(mib):
    return pltpu.CompilerParams(vmem_limit_bytes=mib * MIB)


def pack_kernel(embed_ref, margin_ref, out_ref, spread):
    pieces, message, _ = out_ref.shape
    rows = embed_ref.shape[0] // pieces
    halves = embed_ref.shape[1] // LANES
    margin_rows = margin_ref.shape[1] // LANES
    for r in range(margin_rows):
        spread[r : r + 1, :] = margin_ref[0:1, r * LANES : (r + 1) * LANES].astype(jnp.float32)
    offsets = spread[...].astype(jnp.bfloat16)
    for s in range(pieces):
        for h in range(halves):
            out_ref[s, h * rows : (h + 1) * rows, :] = embed_ref[
                s * rows : (s + 1) * rows, h * LANES : (h + 1) * LANES
            ].astype(jnp.bfloat16)
        out_ref[s, halves * rows :, :] = offsets


def pick_kernel(orders, slot_ref, held_ref, out_ref, offsets_ref, copied):
    requests, piece, _ = out_ref.shape
    copies = []
    for r in range(requests):
        slot = slot_ref[orders.fetch[r]]
        copies.append(
            pltpu.make_async_copy(
                held_ref.at[slot, pl.ds(0, piece), :], out_ref.at[r], copied.at[r]
            )
        )
        copies[-1].start()
    offsets_ref[...] = held_ref[:, piece:, :]
    for copy in copies:
        copy.wait()


def tile_kernel(
    orders, place_ref, counts_ref, arrived_ref, mine_ref, other_ref, out_ref, row_off, col_off
):
    requests, rows, width = out_ref.shape
    owners = requests // orders.planes
    halves = width // LANES
    block = counts_ref.shape[0]

    def vectors(pieces, plane):
        places = [orders.fetch.index(orders.holder(p, plane)) for p in pieces]
        parts = [
            jnp.concatenate([arrived_ref[j, h * rows : (h + 1) * rows, :] for j in places], axis=0)
            for h in range(halves)
        ]
        return jnp.concatenate(parts, axis=1)

    def deal(gradient, pieces, plane):
        coded = code(gradient).astype(jnp.bfloat16)
        for q, p in enumerate(pieces):
            out_ref[orders.back.index(orders.holder(p, plane))] = coded[q * rows : (q + 1) * rows, :]

    plane = place_ref[0]
    row_slot = place_ref[1]
    col_slot = place_ref[2]
    row_m = jnp.where(plane == 0, mine_ref[row_slot], other_ref[row_slot]).astype(jnp.float32)
    col_m = jnp.where(plane == 0, other_ref[col_slot], mine_ref[col_slot]).astype(jnp.float32)
    turned = jnp.transpose(row_m)
    for r in range(block // LANES):
        row_off[r * LANES : (r + 1) * LANES, :] = turned[:, r : r + 1]
        col_off[:, r * LANES : (r + 1) * LANES] = col_m[r : r + 1, :]
    cols = vectors(range(owners), 1)
    pieces = ROWS // rows
    col_sum = None
    for step in range(block // ROWS):
        here = slice(step * ROWS, (step + 1) * ROWS)
        there = range(step * pieces, (step + 1) * pieces)
        row_vectors = vectors(there, 0)
        scores = lax.dot_general(
            row_vectors, cols, (((1,), (1,)), ((), ())), preferred_element_type=jnp.float32
        )
        shifted = scores + (row_off[here, :] + col_off[...])
        tile_counts = counts_ref[here, :].astype(jnp.float32)
        counted = jnp.maximum(tile_counts, 1.0)
        confidence = conf_base + conf_scale * (counted * lax.rsqrt(counted))
        fitted = confidence * (shifted - jnp.log(counted))
        hinge = 0.5 + 0.5 * jnp.tanh(0.5 * shifted)
        cell_grad = jnp.where(tile_counts > 0, fitted, hinge).astype(jnp.bfloat16)
        row_gradient = jnp.dot(cell_grad, cols, preferred_element_type=jnp.float32)
        deal(row_gradient, there, 0)
        part = lax.dot_general(
            cell_grad, row_vectors, (((0,), (0,)), ((), ())), preferred_element_type=jnp.float32
        )
        col_sum = part if step == 0 else col_sum + part
    deal(col_sum, range(owners), 1)


def sum_kernel(orders, slot_ref, returned_ref, out_ref, total):
    total[...] = jnp.zeros_like(total)
    for r in range(returned_ref.shape[0]):
        total[slot_ref[orders.back[r]]] += decode(returned_ref[r])
    for s, chip in enumerate(orders.collect):
        out_ref[s] = code(total[orders.chip_place[chip]]).astype(jnp.bfloat16)


def update_kernel(
    orders, sums_ref, embed_ref, accum_ref, new_embed_ref, new_accum_ref, embed_v, accum_v, copied
):
    pieces, rows, width = sums_ref.shape
    steps = copied.shape[1]
    copies = []
    for step in range(steps):
        some = pieces // steps
        here = pl.ds(step * some * rows, some * rows)
        held = [orders.collect.index(orders.chips[p]) for p in range(step * some, (step + 1) * some)]
        gradient = decode(jnp.concatenate([sums_ref[p] for p in held], axis=0))
        new_accum = accum_ref[here, :] + gradient * gradient
        accum_v[here, :] = new_accum
        embed_v[here, :] = embed_ref[here, :] - learn_rate * gradient * lax.rsqrt(new_accum)
        for k, (new_v, new_ref) in enumerate(((accum_v, new_accum_ref), (embed_v, new_embed_ref))):
            copies.append(
                pltpu.make_async_copy(new_v.at[here, :], new_ref.at[here, :], copied.at[k, step])
            )
            copies[-1].start()
    for copy in copies:
        copy.wait()


def per_device(counts, tile_list, owner_map, embed, accum, margins):
    owners = lax.axis_size("blk")
    requests = owners * lax.axis_size("rep")
    plane = lax.axis_index("rep")
    block, width = embed.shape[1:]
    rows = block // owners
    halves = width // LANES
    margin_rows = block // LANES
    smem = pl.BlockSpec(memory_space=pltpu.SMEM)
    vmem = pl.BlockSpec(memory_space=pltpu.VMEM)
    f32, bf16 = jnp.float32, jnp.bfloat16

    orders = Orders(owners, requests)
    places = jnp.asarray(orders.chip_place, jnp.int32)[owner_map]
    wanted = jnp.stack([places[k][tile_list[:, k]] for k in range(2)])
    slot_of = wanted[plane]
    me = lax.axis_index("blk") * lax.axis_size("rep") + plane
    place = jnp.concatenate([plane[None], wanted[:, me]]).astype(jnp.int32)

    steps = 2
    outgoing = pl.pallas_call(
        pack_kernel,
        grid=(steps,),
        in_specs=[
            pl.BlockSpec((block // steps, width), lambda i: (i, 0)),
            pl.BlockSpec((1, block), lambda i: (0, 0)),
        ],
        out_specs=pl.BlockSpec((owners // steps, halves * rows + margin_rows, LANES), lambda i: (i, 0, 0)),
        out_shape=jax.ShapeDtypeStruct((owners, halves * rows + margin_rows, LANES), bf16),
        scratch_shapes=[pltpu.VMEM((margin_rows, LANES), f32)],
        compiler_params=params(60),
        name="pack",
    )(embed[0], margins)
    held = swap_chips(outgoing, orders.chips)
    picked, offsets = pl.pallas_call(
        functools.partial(pick_kernel, orders),
        in_specs=[smem, vmem],
        out_specs=(pl.BlockSpec(memory_space=pl.ANY), vmem),
        out_shape=(
            jax.ShapeDtypeStruct((requests, halves * rows, LANES), bf16),
            jax.ShapeDtypeStruct((owners, margin_rows, LANES), bf16),
        ),
        scratch_shapes=[pltpu.SemaphoreType.DMA((requests,))],
        compiler_params=params(16),
        name="pick",
    )(slot_of, held)
    other_offsets = lax.ppermute(offsets, "rep", [(0, 1), (1, 0)])
    arrived = swap_all(picked, orders.fetch)
    partials = pl.pallas_call(
        functools.partial(tile_kernel, orders),
        in_specs=[smem] + [vmem] * 4,
        out_shape=jax.ShapeDtypeStruct((requests, rows, width), bf16),
        scratch_shapes=[
            pltpu.VMEM((block, 1), f32),
            pltpu.VMEM((1, block), f32),
        ],
        compiler_params=params(24),
        name="tile",
    )(place, counts[0].astype(bf16), arrived, offsets, other_offsets)
    returned = swap_all(partials, orders.back)
    sums = pl.pallas_call(
        functools.partial(sum_kernel, orders),
        in_specs=[smem, vmem],
        out_shape=jax.ShapeDtypeStruct((owners, rows, width), bf16),
        scratch_shapes=[pltpu.VMEM((owners, rows, width), f32)],
        compiler_params=params(16),
        name="sum",
    )(slot_of, returned)
    gradient = swap_chips(sums, orders.collect)
    new_embed, new_accum = pl.pallas_call(
        functools.partial(update_kernel, orders),
        in_specs=[vmem] * 3,
        out_specs=(pl.BlockSpec(memory_space=pl.ANY),) * 2,
        out_shape=(jax.ShapeDtypeStruct((block, width), f32),) * 2,
        scratch_shapes=[
            pltpu.VMEM((block, width), f32),
            pltpu.VMEM((block, width), f32),
            pltpu.SemaphoreType.DMA((2, 4)),
        ],
        compiler_params=params(16),
        name="update",
    )(gradient, embed[0], accum[0])
    return (new_embed[None], new_accum[None])


def solution(mesh):
    in_specs = (
        P(("blk", "rep"), None, None),
        P(),
        P(),
        P("rep", "blk", None),
        P("rep", "blk", None),
        P("rep", "blk"),
    )
    out_specs = (P("rep", "blk", None), P("rep", "blk", None))
    return jax.shard_map(
        per_device, mesh=mesh, in_specs=in_specs, out_specs=out_specs, check_vma=False
    )
```

```python
import functools

import jax
import jax.numpy as jnp
from jax import lax
from jax.experimental import pallas as pl
from jax.experimental.pallas import tpu as pltpu
from jax.sharding import PartitionSpec as P

learn_rate = 0.05
conf_base = 0.1
conf_scale = 0.25

LANES = 128

SPREAD_ORDER = (
    7, 12, 5, 15, 10, 3, 14, 9, 13, 6, 8, 2, 1, 0, 11, 4,
)
FETCH_ORDER = (
    0, 8, 16, 24, 4, 12, 19, 28, 1, 9, 17, 25, 29, 21, 13, 5,
    2, 10, 18, 26, 6, 14, 22, 30, 3, 11, 20, 27, 7, 15, 23, 31,
)
RETURN_ORDER = (
    0, 1, 15, 14, 13, 12, 2, 9, 10, 8, 7, 6, 5, 4, 3, 11,
    16, 17, 18, 19, 20, 21, 22, 23, 24, 25, 26, 27, 28, 29, 30, 31,
)
COLLECT_ORDER = (
    8, 10, 3, 14, 2, 11, 13, 4, 6, 12, 5, 7, 1, 0, 15, 9,
)


class Orders:
    def __init__(self, owners, requests):
        tuned = owners == len(SPREAD_ORDER) and requests == len(RETURN_ORDER)
        self.chips = SPREAD_ORDER if tuned else tuple(range(owners))
        self.collect = COLLECT_ORDER if tuned else tuple(range(owners))
        self.fetch = FETCH_ORDER if tuned else tuple(range(requests))
        self.back = RETURN_ORDER if tuned else tuple(range(requests))
        self.chip_place = tuple(self.chips.index(c) for c in range(owners))
        self.planes = requests // owners

    def holder(self, piece, plane):
        return self.chips[piece] * self.planes + plane


def swap_chips(x, chips):
    return lax.all_to_all(
        x, "blk", split_axis=0, concat_axis=0, tiled=True, axis_index_groups=[list(chips)]
    )


def swap_all(x, devices):
    return lax.all_to_all(
        x,
        ("blk", "rep"),
        split_axis=0,
        concat_axis=0,
        tiled=True,
        axis_index_groups=[list(devices)],
    )

ROWS = 256
MIB = 1024 * 1024


def code(v):
    return (v * v) * (v * jnp.abs(v))


def decode(x):
    x = x.astype(jnp.float32)
    size = jnp.maximum(jnp.abs(x), 1e-37)
    once = lax.rsqrt(size)
    return (x * once) * lax.rsqrt(size * once)


def params(mib):
    return pltpu.CompilerParams(vmem_limit_bytes=mib * MIB)


def pack_kernel(embed_ref, margin_ref, out_ref, spread):
    pieces, message, _ = out_ref.shape
    rows = embed_ref.shape[0] // pieces
    halves = embed_ref.shape[1] // LANES
    margin_rows = margin_ref.shape[1] // LANES
    for r in range(margin_rows):
        spread[r : r + 1, :] = margin_ref[0:1, r * LANES : (r + 1) * LANES].astype(jnp.float32)
    offsets = spread[...].astype(jnp.bfloat16)
    for s in range(pieces):
        for h in range(halves):
            out_ref[s, h * rows : (h + 1) * rows, :] = embed_ref[
                s * rows : (s + 1) * rows, h * LANES : (h + 1) * LANES
            ].astype(jnp.bfloat16)
        out_ref[s, halves * rows :, :] = offsets


def pick_kernel(orders, slot_ref, held_ref, out_ref, offsets_ref, copied):
    requests, piece, _ = out_ref.shape
    copies = []
    for r in range(requests):
        slot = slot_ref[orders.fetch[r]]
        copies.append(
            pltpu.make_async_copy(
                held_ref.at[slot, pl.ds(0, piece), :], out_ref.at[r], copied.at[r]
            )
        )
        copies[-1].start()
    offsets_ref[...] = held_ref[:, piece:, :]
    for copy in copies:
        copy.wait()


def tile_kernel(
    orders, place_ref, counts_ref, arrived_ref, mine_ref, other_ref, out_ref, row_off, col_off
):
    requests, rows, width = out_ref.shape
    owners = requests // orders.planes
    halves = width // LANES
    block = counts_ref.shape[0]

    def vectors(pieces, plane):
        places = [orders.fetch.index(orders.holder(p, plane)) for p in pieces]
        parts = [
            jnp.concatenate([arrived_ref[j, h * rows : (h + 1) * rows, :] for j in places], axis=0)
            for h in range(halves)
        ]
        return jnp.concatenate(parts, axis=1)

    def deal(gradient, pieces, plane):
        coded = code(gradient).astype(jnp.bfloat16)
        for q, p in enumerate(pieces):
            out_ref[orders.back.index(orders.holder(p, plane))] = coded[q * rows : (q + 1) * rows, :]

    plane = place_ref[0]
    row_slot = place_ref[1]
    col_slot = place_ref[2]
    row_m = jnp.where(plane == 0, mine_ref[row_slot], other_ref[row_slot]).astype(jnp.float32)
    col_m = jnp.where(plane == 0, other_ref[col_slot], mine_ref[col_slot]).astype(jnp.float32)
    turned = jnp.transpose(row_m)
    for r in range(block // LANES):
        row_off[r * LANES : (r + 1) * LANES, :] = turned[:, r : r + 1]
        col_off[:, r * LANES : (r + 1) * LANES] = col_m[r : r + 1, :]
    cols = vectors(range(owners), 1)
    pieces = ROWS // rows
    col_sum = None
    for step in range(block // ROWS):
        here = slice(step * ROWS, (step + 1) * ROWS)
        there = range(step * pieces, (step + 1) * pieces)
        row_vectors = vectors(there, 0)
        scores = lax.dot_general(
            row_vectors, cols, (((1,), (1,)), ((), ())), preferred_element_type=jnp.float32
        )
        shifted = scores + (row_off[here, :] + col_off[...])
        tile_counts = counts_ref[here, :].astype(jnp.float32)
        counted = jnp.maximum(tile_counts, 1.0)
        confidence = conf_base + conf_scale * (counted * lax.rsqrt(counted))
        fitted = confidence * (shifted - jnp.log(counted))
        hinge = 0.5 + 0.5 * jnp.tanh(0.5 * shifted)
        cell_grad = jnp.where(tile_counts > 0, fitted, hinge).astype(jnp.bfloat16)
        row_gradient = jnp.dot(cell_grad, cols, preferred_element_type=jnp.float32)
        deal(row_gradient, there, 0)
        part = lax.dot_general(
            cell_grad, row_vectors, (((0,), (0,)), ((), ())), preferred_element_type=jnp.float32
        )
        col_sum = part if step == 0 else col_sum + part
    deal(col_sum, range(owners), 1)


def sum_kernel(orders, slot_ref, returned_ref, out_ref, total):
    total[...] = jnp.zeros_like(total)
    for r in range(returned_ref.shape[0]):
        total[slot_ref[orders.back[r]]] += decode(returned_ref[r])
    for s, chip in enumerate(orders.collect):
        out_ref[s] = code(total[orders.chip_place[chip]]).astype(jnp.bfloat16)


def update_kernel(
    orders, sums_ref, embed_ref, accum_ref, new_embed_ref, new_accum_ref, embed_v, accum_v, copied
):
    pieces, rows, width = sums_ref.shape
    steps = copied.shape[1]
    copies = []
    for step in range(steps):
        some = pieces // steps
        here = pl.ds(step * some * rows, some * rows)
        held = [orders.collect.index(orders.chips[p]) for p in range(step * some, (step + 1) * some)]
        gradient = decode(jnp.concatenate([sums_ref[p] for p in held], axis=0))
        new_accum = accum_ref[here, :] + gradient * gradient
        accum_v[here, :] = new_accum
        embed_v[here, :] = embed_ref[here, :] - learn_rate * gradient * lax.rsqrt(new_accum)
        for k, (new_v, new_ref) in enumerate(((accum_v, new_accum_ref), (embed_v, new_embed_ref))):
            copies.append(
                pltpu.make_async_copy(new_v.at[here, :], new_ref.at[here, :], copied.at[k, step])
            )
            copies[-1].start()
    for copy in copies:
        copy.wait()


def per_device(counts, tile_list, owner_map, embed, accum, margins):
    owners = lax.axis_size("blk")
    requests = owners * lax.axis_size("rep")
    plane = lax.axis_index("rep")
    block, width = embed.shape[1:]
    rows = block // owners
    halves = width // LANES
    margin_rows = block // LANES
    smem = pl.BlockSpec(memory_space=pltpu.SMEM)
    vmem = pl.BlockSpec(memory_space=pltpu.VMEM)
    f32, bf16 = jnp.float32, jnp.bfloat16

    orders = Orders(owners, requests)
    places = jnp.asarray(orders.chip_place, jnp.int32)[owner_map]
    wanted = jnp.stack([places[k][tile_list[:, k]] for k in range(2)])
    slot_of = wanted[plane]
    me = lax.axis_index("blk") * lax.axis_size("rep") + plane
    place = jnp.concatenate([plane[None], wanted[:, me]]).astype(jnp.int32)

    steps = 2
    outgoing = pl.pallas_call(
        pack_kernel,
        grid=(steps,),
        in_specs=[
            pl.BlockSpec((block // steps, width), lambda i: (i, 0)),
            pl.BlockSpec((1, block), lambda i: (0, 0)),
        ],
        out_specs=pl.BlockSpec((owners // steps, halves * rows + margin_rows, LANES), lambda i: (i, 0, 0)),
        out_shape=jax.ShapeDtypeStruct((owners, halves * rows + margin_rows, LANES), bf16),
        scratch_shapes=[pltpu.VMEM((margin_rows, LANES), f32)],
        compiler_params=params(60),
        name="pack",
    )(embed[0], margins)
    held = swap_chips(outgoing, orders.chips)
    picked, offsets = pl.pallas_call(
        functools.partial(pick_kernel, orders),
        in_specs=[smem, vmem],
        out_specs=(pl.BlockSpec(memory_space=pl.ANY), vmem),
        out_shape=(
            jax.ShapeDtypeStruct((requests, halves * rows, LANES), bf16),
            jax.ShapeDtypeStruct((owners, margin_rows, LANES), bf16),
        ),
        scratch_shapes=[pltpu.SemaphoreType.DMA((requests,))],
        compiler_params=params(16),
        name="pick",
    )(slot_of, held)
    other_offsets = lax.ppermute(offsets, "rep", [(0, 1), (1, 0)])
    arrived = swap_all(picked, orders.fetch)
    partials = pl.pallas_call(
        functools.partial(tile_kernel, orders),
        in_specs=[smem] + [vmem] * 4,
        out_shape=jax.ShapeDtypeStruct((requests, rows, width), bf16),
        scratch_shapes=[
            pltpu.VMEM((block, 1), f32),
            pltpu.VMEM((1, block), f32),
        ],
        compiler_params=params(24),
        name="tile",
    )(place, counts[0].astype(bf16), arrived, offsets, other_offsets)
    returned = swap_all(partials, orders.back)
    sums = pl.pallas_call(
        functools.partial(sum_kernel, orders),
        in_specs=[smem, vmem],
        out_shape=jax.ShapeDtypeStruct((owners, rows, width), bf16),
        scratch_shapes=[pltpu.VMEM((owners, rows, width), f32)],
        compiler_params=params(16),
        name="sum",
    )(slot_of, returned)
    gradient = swap_chips(sums, orders.collect)
    new_embed, new_accum = pl.pallas_call(
        functools.partial(update_kernel, orders),
        in_specs=[vmem] * 3,
        out_specs=(pl.BlockSpec(memory_space=pl.ANY),) * 2,
        out_shape=(jax.ShapeDtypeStruct((block, width), f32),) * 2,
        scratch_shapes=[
            pltpu.VMEM((block, width), f32),
            pltpu.VMEM((block, width), f32),
            pltpu.SemaphoreType.DMA((2, 4)),
        ],
        compiler_params=params(16),
        name="update",
    )(gradient, embed[0], accum[0])
    return (new_embed[None], new_accum[None])


def solution(mesh):
    in_specs = (
        P(("blk", "rep"), None, None),
        P(),
        P(),
        P("rep", "blk", None),
        P("rep", "blk", None),
        P("rep", "blk"),
    )
    out_specs = (P("rep", "blk", None), P("rep", "blk", None))
    return jax.shard_map(
        per_device, mesh=mesh, in_specs=in_specs, out_specs=out_specs, check_vma=False
    )
```

```python
import functools

import jax
import jax.numpy as jnp
from jax import lax
from jax.experimental import pallas as pl
from jax.experimental.pallas import tpu as pltpu
from jax.sharding import PartitionSpec as P

learn_rate = 0.05
conf_base = 0.1
conf_scale = 0.25

LANES = 128

SPREAD_ORDER = (
    7, 3, 13, 15, 10, 12, 2, 11, 5, 6, 8, 14, 1, 0, 9, 4,
)
FETCH_ORDER = (
    0, 8, 16, 24, 4, 12, 19, 28, 1, 9, 17, 25, 29, 21, 13, 5,
    2, 10, 18, 26, 6, 14, 22, 30, 3, 11, 20, 27, 7, 15, 23, 31,
)
RETURN_ORDER = (
    0, 1, 15, 14, 13, 12, 2, 9, 10, 8, 7, 6, 5, 4, 3, 11,
    16, 17, 18, 19, 20, 21, 22, 23, 24, 25, 26, 27, 28, 29, 30, 31,
)
COLLECT_ORDER = (
    8, 10, 3, 14, 2, 11, 13, 4, 6, 12, 5, 7, 1, 0, 15, 9,
)


class Orders:
    def __init__(self, owners, requests):
        tuned = owners == len(SPREAD_ORDER) and requests == len(RETURN_ORDER)
        self.chips = SPREAD_ORDER if tuned else tuple(range(owners))
        self.collect = COLLECT_ORDER if tuned else tuple(range(owners))
        self.fetch = FETCH_ORDER if tuned else tuple(range(requests))
        self.back = RETURN_ORDER if tuned else tuple(range(requests))
        self.chip_place = tuple(self.chips.index(c) for c in range(owners))
        self.planes = requests // owners

    def holder(self, piece, plane):
        return self.chips[piece] * self.planes + plane


def swap_chips(x, chips):
    return lax.all_to_all(
        x, "blk", split_axis=0, concat_axis=0, tiled=True, axis_index_groups=[list(chips)]
    )


def swap_all(x, devices):
    return lax.all_to_all(
        x,
        ("blk", "rep"),
        split_axis=0,
        concat_axis=0,
        tiled=True,
        axis_index_groups=[list(devices)],
    )

ROWS = 256
MIB = 1024 * 1024


def code(v):
    return (v * v) * (v * jnp.abs(v))


def decode(x):
    x = x.astype(jnp.float32)
    size = jnp.maximum(jnp.abs(x), 1e-37)
    once = lax.rsqrt(size)
    return (x * once) * lax.rsqrt(size * once)


def params(mib):
    return pltpu.CompilerParams(vmem_limit_bytes=mib * MIB)


def pack_kernel(embed_ref, margin_ref, out_ref, spread):
    pieces, message, _ = out_ref.shape
    rows = embed_ref.shape[0] // pieces
    halves = embed_ref.shape[1] // LANES
    margin_rows = margin_ref.shape[1] // LANES
    for r in range(margin_rows):
        spread[r : r + 1, :] = margin_ref[0:1, r * LANES : (r + 1) * LANES].astype(jnp.float32)
    offsets = spread[...].astype(jnp.bfloat16)
    for s in range(pieces):
        for h in range(halves):
            out_ref[s, h * rows : (h + 1) * rows, :] = embed_ref[
                s * rows : (s + 1) * rows, h * LANES : (h + 1) * LANES
            ].astype(jnp.bfloat16)
        out_ref[s, halves * rows :, :] = offsets


def pick_kernel(orders, slot_ref, held_ref, out_ref, offsets_ref, copied):
    requests, piece, _ = out_ref.shape
    copies = []
    for r in range(requests):
        slot = slot_ref[orders.fetch[r]]
        copies.append(
            pltpu.make_async_copy(
                held_ref.at[slot, pl.ds(0, piece), :], out_ref.at[r], copied.at[r]
            )
        )
        copies[-1].start()
    offsets_ref[...] = held_ref[:, piece:, :]
    for copy in copies:
        copy.wait()


def tile_kernel(
    orders, place_ref, counts_ref, arrived_ref, mine_ref, other_ref, out_ref, row_off, col_off
):
    requests, rows, width = out_ref.shape
    owners = requests // orders.planes
    halves = width // LANES
    block = counts_ref.shape[0]

    def vectors(pieces, plane):
        places = [orders.fetch.index(orders.holder(p, plane)) for p in pieces]
        parts = [
            jnp.concatenate([arrived_ref[j, h * rows : (h + 1) * rows, :] for j in places], axis=0)
            for h in range(halves)
        ]
        return jnp.concatenate(parts, axis=1)

    def deal(gradient, pieces, plane):
        coded = code(gradient).astype(jnp.bfloat16)
        for q, p in enumerate(pieces):
            out_ref[orders.back.index(orders.holder(p, plane))] = coded[q * rows : (q + 1) * rows, :]

    plane = place_ref[0]
    row_slot = place_ref[1]
    col_slot = place_ref[2]
    row_m = jnp.where(plane == 0, mine_ref[row_slot], other_ref[row_slot]).astype(jnp.float32)
    col_m = jnp.where(plane == 0, other_ref[col_slot], mine_ref[col_slot]).astype(jnp.float32)
    turned = jnp.transpose(row_m)
    for r in range(block // LANES):
        row_off[r * LANES : (r + 1) * LANES, :] = turned[:, r : r + 1]
        col_off[:, r * LANES : (r + 1) * LANES] = col_m[r : r + 1, :]
    cols = vectors(range(owners), 1)
    pieces = ROWS // rows
    col_sum = None
    for step in range(block // ROWS):
        here = slice(step * ROWS, (step + 1) * ROWS)
        there = range(step * pieces, (step + 1) * pieces)
        row_vectors = vectors(there, 0)
        scores = lax.dot_general(
            row_vectors, cols, (((1,), (1,)), ((), ())), preferred_element_type=jnp.float32
        )
        shifted = scores + (row_off[here, :] + col_off[...])
        tile_counts = counts_ref[here, :].astype(jnp.float32)
        counted = jnp.maximum(tile_counts, 1.0)
        confidence = conf_base + conf_scale * (counted * lax.rsqrt(counted))
        fitted = confidence * (shifted - jnp.log(counted))
        hinge = 0.5 + 0.5 * jnp.tanh(0.5 * shifted)
        cell_grad = jnp.where(tile_counts > 0, fitted, hinge).astype(jnp.bfloat16)
        row_gradient = jnp.dot(cell_grad, cols, preferred_element_type=jnp.float32)
        deal(row_gradient, there, 0)
        part = lax.dot_general(
            cell_grad, row_vectors, (((0,), (0,)), ((), ())), preferred_element_type=jnp.float32
        )
        col_sum = part if step == 0 else col_sum + part
    deal(col_sum, range(owners), 1)


def sum_kernel(orders, slot_ref, returned_ref, out_ref, total):
    total[...] = jnp.zeros_like(total)
    for r in range(returned_ref.shape[0]):
        total[slot_ref[orders.back[r]]] += decode(returned_ref[r])
    for s, chip in enumerate(orders.collect):
        out_ref[s] = code(total[orders.chip_place[chip]]).astype(jnp.bfloat16)


def update_kernel(
    orders, sums_ref, embed_ref, accum_ref, new_embed_ref, new_accum_ref, embed_v, accum_v, copied
):
    pieces, rows, width = sums_ref.shape
    steps = copied.shape[1]
    copies = []
    for step in range(steps):
        some = pieces // steps
        here = pl.ds(step * some * rows, some * rows)
        held = [orders.collect.index(orders.chips[p]) for p in range(step * some, (step + 1) * some)]
        gradient = decode(jnp.concatenate([sums_ref[p] for p in held], axis=0))
        new_accum = accum_ref[here, :] + gradient * gradient
        accum_v[here, :] = new_accum
        embed_v[here, :] = embed_ref[here, :] - learn_rate * gradient * lax.rsqrt(new_accum)
        for k, (new_v, new_ref) in enumerate(((accum_v, new_accum_ref), (embed_v, new_embed_ref))):
            copies.append(
                pltpu.make_async_copy(new_v.at[here, :], new_ref.at[here, :], copied.at[k, step])
            )
            copies[-1].start()
    for copy in copies:
        copy.wait()


def per_device(counts, tile_list, owner_map, embed, accum, margins):
    owners = lax.axis_size("blk")
    requests = owners * lax.axis_size("rep")
    plane = lax.axis_index("rep")
    block, width = embed.shape[1:]
    rows = block // owners
    halves = width // LANES
    margin_rows = block // LANES
    smem = pl.BlockSpec(memory_space=pltpu.SMEM)
    vmem = pl.BlockSpec(memory_space=pltpu.VMEM)
    f32, bf16 = jnp.float32, jnp.bfloat16

    orders = Orders(owners, requests)
    places = jnp.asarray(orders.chip_place, jnp.int32)[owner_map]
    wanted = jnp.stack([places[k][tile_list[:, k]] for k in range(2)])
    slot_of = wanted[plane]
    me = lax.axis_index("blk") * lax.axis_size("rep") + plane
    place = jnp.concatenate([plane[None], wanted[:, me]]).astype(jnp.int32)

    steps = 2
    outgoing = pl.pallas_call(
        pack_kernel,
        grid=(steps,),
        in_specs=[
            pl.BlockSpec((block // steps, width), lambda i: (i, 0)),
            pl.BlockSpec((1, block), lambda i: (0, 0)),
        ],
        out_specs=pl.BlockSpec((owners // steps, halves * rows + margin_rows, LANES), lambda i: (i, 0, 0)),
        out_shape=jax.ShapeDtypeStruct((owners, halves * rows + margin_rows, LANES), bf16),
        scratch_shapes=[pltpu.VMEM((margin_rows, LANES), f32)],
        compiler_params=params(60),
        name="pack",
    )(embed[0], margins)
    held = swap_chips(outgoing, orders.chips)
    picked, offsets = pl.pallas_call(
        functools.partial(pick_kernel, orders),
        in_specs=[smem, vmem],
        out_specs=(pl.BlockSpec(memory_space=pl.ANY), vmem),
        out_shape=(
            jax.ShapeDtypeStruct((requests, halves * rows, LANES), bf16),
            jax.ShapeDtypeStruct((owners, margin_rows, LANES), bf16),
        ),
        scratch_shapes=[pltpu.SemaphoreType.DMA((requests,))],
        compiler_params=params(16),
        name="pick",
    )(slot_of, held)
    other_offsets = lax.ppermute(offsets, "rep", [(0, 1), (1, 0)])
    arrived = swap_all(picked, orders.fetch)
    partials = pl.pallas_call(
        functools.partial(tile_kernel, orders),
        in_specs=[smem] + [vmem] * 4,
        out_shape=jax.ShapeDtypeStruct((requests, rows, width), bf16),
        scratch_shapes=[
            pltpu.VMEM((block, 1), f32),
            pltpu.VMEM((1, block), f32),
        ],
        compiler_params=params(24),
        name="tile",
    )(place, counts[0].astype(bf16), arrived, offsets, other_offsets)
    returned = swap_all(partials, orders.back)
    sums = pl.pallas_call(
        functools.partial(sum_kernel, orders),
        in_specs=[smem, vmem],
        out_shape=jax.ShapeDtypeStruct((owners, rows, width), bf16),
        scratch_shapes=[pltpu.VMEM((owners, rows, width), f32)],
        compiler_params=params(16),
        name="sum",
    )(slot_of, returned)
    gradient = swap_chips(sums, orders.collect)
    new_embed, new_accum = pl.pallas_call(
        functools.partial(update_kernel, orders),
        in_specs=[vmem] * 3,
        out_specs=(pl.BlockSpec(memory_space=pl.ANY),) * 2,
        out_shape=(jax.ShapeDtypeStruct((block, width), f32),) * 2,
        scratch_shapes=[
            pltpu.VMEM((block, width), f32),
            pltpu.VMEM((block, width), f32),
            pltpu.SemaphoreType.DMA((2, 4)),
        ],
        compiler_params=params(16),
        name="update",
    )(gradient, embed[0], accum[0])
    return (new_embed[None], new_accum[None])


def solution(mesh):
    in_specs = (
        P(("blk", "rep"), None, None),
        P(),
        P(),
        P("rep", "blk", None),
        P("rep", "blk", None),
        P("rep", "blk"),
    )
    out_specs = (P("rep", "blk", None), P("rep", "blk", None))
    return jax.shard_map(
        per_device, mesh=mesh, in_specs=in_specs, out_specs=out_specs, check_vma=False
    )
```
